128 devices in a mesh: scene: 128 (over x, z, y, core).
Axes of the slice: x: 4, y: 4, z: 4, core: 2. Of those that a mesh axis runs over, the one named last changes fastest.
Arguments:
- first_scene: int32 [3072], P('scene'), may hold values from 0 to 1023, as said below
- second_scene: int32 [3072], P('scene'), may hold values from 0 to 1023, as said below
- rad_first: bfloat16 [3072, 224, 128], P('scene'), may hold values from 0.5 to 1.5
- rad_second: bfloat16 [3072, 224, 128], P('scene'), may hold values from 0.5 to 1.5
- pos_first: int32 [3072, 128], P('scene'), may hold values from 0 to 1023
- pos_second: int32 [3072, 128], P('scene'), may hold values from 0 to 1023
- prior_weight: float32 [1024], P('scene'), may hold values from 1 to 10
Outputs:
- solution: float32 [1024, 28672], P('scene')
- residual: float32 [1024, 28672], P('scene')
The draws below stay inside these ranges and needn't reach their ends.
Inputs may be any that keep to these rules, and one draw needn't show every extreme that they name: first_scene of every pair lies among the 8 scenes of the device that holds the pair, in strip order. second_scene equals (first_scene + k) modulo 1024 for some k from 1 to 8; the strip closes on itself, and k = 8 occurs on every device.
All inputs are finite; a program needn't handle non-finite values.
Results may differ from the reference program's by a relative error of at most 0.0003.
Values sent between devices are 32-bit elements; how exact they have to be, the bound alone decides.
A program may use at most 128 MiB of HBM per device.

```python
import math
import jax
import jax.numpy as jnp
from jax import lax

BANDS = 224
TERMS = 64
COLS = 1024
SAMPLES = 128
SCENE_DEV = 8
ITERS = 2
PAIR_DEV = 24
SCENES = 1024
PAIRS = 3072
N_SCENE = 128


def pair_scenes(key):
    inner = jax.random.fold_in(key, 4711)
    key_local, key_ahead = jax.random.split(inner)
    slots = jnp.arange(PAIRS, dtype=jnp.int32)
    local = jax.random.randint(key_local, (PAIRS,), 0, SCENE_DEV, dtype=jnp.int32)
    ahead = jax.random.randint(key_ahead, (PAIRS,), 1, SCENE_DEV + 1, dtype=jnp.int32)
    ahead = jnp.where(slots % PAIR_DEV == 0, SCENE_DEV, ahead)
    first = slots // PAIR_DEV * SCENE_DEV + local
    second = jnp.mod(first + ahead, SCENES)
    return (first.astype(jnp.int32), second.astype(jnp.int32))


def draw_first_scene(key, part):
    return pair_scenes(key)[0]


def draw_second_scene(key, part):
    return pair_scenes(key)[1]


def place_ends(array, key, smallest, largest):
    place = [jax.random.randint(jax.random.fold_in(key, axis), (), 0, length) for axis, length in enumerate(array.shape)]
    main_axis = array.shape.index(max(array.shape))
    neighbour = place[:main_axis] + [(place[main_axis] + 1) % array.shape[main_axis]] + place[main_axis + 1:]
    return array.at[tuple(place)].set(smallest).at[tuple(neighbour)].set(largest)


def levels(own_key, dims, shards, low, high):
    def one(axis_at, shards_of):
        heights = jax.random.uniform(jax.random.fold_in(jax.random.fold_in(own_key, 6), axis_at), (shards_of,), jnp.float32, low / len(shards), high / len(shards))
        return jnp.repeat(jnp.exp(heights), dims[axis_at] // shards_of).reshape((-1,) + (1,) * (len(dims) - axis_at - 1))

    loudness = one(*shards[0])
    for cut in shards[1:]:
        loudness = loudness * one(*cut)
    return loudness


def setup_inputs(seed: int = 0) -> dict:
    splits = jax.random.split(jax.random.key(seed), 8)
    first_scene = draw_first_scene(jax.random.fold_in(splits[7], 71), 0)
    second_scene = draw_second_scene(jax.random.fold_in(splits[7], 71), 0)
    rad_first = jnp.clip(0.5 + 1.0 * jax.random.uniform(splits[2], (PAIRS, BANDS, SAMPLES), jnp.float32) ** levels(splits[2], (PAIRS, BANDS, SAMPLES), ((0, 128),), -0.2, 0.2), 0.5, 1.5).astype(jnp.bfloat16)
    rad_second = jnp.clip(0.5 + 1.0 * jax.random.uniform(splits[3], (PAIRS, BANDS, SAMPLES), jnp.float32) ** levels(splits[3], (PAIRS, BANDS, SAMPLES), ((0, 128),), -0.2, 0.2), 0.5, 1.5).astype(jnp.bfloat16)
    pos_first = place_ends(jax.random.randint(splits[4], (PAIRS, SAMPLES), 0, COLS), jax.random.fold_in(splits[4], 1), 0, COLS - 1).astype(jnp.int32)
    pos_second = place_ends(jax.random.randint(splits[5], (PAIRS, SAMPLES), 0, COLS), jax.random.fold_in(splits[5], 1), 0, COLS - 1).astype(jnp.int32)
    prior_weight = jnp.clip(jnp.exp(math.log(10.0) - 2.3025851 * jax.random.uniform(splits[6], (SCENES,), jnp.float32) ** levels(splits[6], (SCENES,), ((0, 128),), -0.2, 0.2)), 1.0, 10.0)
    return dict(first_scene=first_scene, second_scene=second_scene, rad_first=rad_first, rad_second=rad_second, pos_first=pos_first, pos_second=pos_second, prior_weight=prior_weight)


HIGH = lax.Precision.HIGHEST

def legendre(pos):
    t = pos.astype(jnp.float32) * (2.0 / (COLS - 1)) - 1.0
    rows = [jnp.ones_like(t), t]
    for k in range(1, TERMS - 1):
        rows.append(((2 * k + 1) * t * rows[k] - k * rows[k - 1]) / (k + 1))
    rows = rows[:TERMS]
    scaled = [rows[k] * (0.0625 * math.sqrt(2 * k + 1)) for k in range(TERMS)]
    return jnp.stack(scaled, axis=-2)

def predict(coef, radiance, phi):
    gain = jnp.einsum('pbk,pks->pbs', coef[:, 0], phi, precision=HIGH)
    offset = jnp.einsum('pbk,pks->pbs', coef[:, 1], phi, precision=HIGH)
    return radiance * gain + offset

def pull(resid, radiance, phi):
    gain = jnp.einsum('pbs,pks->pbk', radiance * resid, phi, precision=HIGH)
    offset = jnp.einsum('pbs,pks->pbk', resid, phi, precision=HIGH)
    return jnp.stack([gain, offset], axis=1)

def diag_terms(radiance, phi):
    square = phi * phi
    gain = jnp.einsum('pbs,pks->pbk', radiance * radiance, square, precision=HIGH)
    offset = jnp.broadcast_to(lax.optimization_barrier(jnp.sum(square, axis=-1))[:, None, :], gain.shape)
    return jnp.stack([gain, offset], axis=1)

def blocked(first_scene, second_scene, rad_first, rad_second, pos_first, pos_second):
    count = N_SCENE
    return (first_scene.reshape(count, PAIR_DEV), second_scene.reshape(count, PAIR_DEV), rad_first.reshape(count, PAIR_DEV, BANDS, SAMPLES), rad_second.reshape(count, PAIR_DEV, BANDS, SAMPLES), pos_first.reshape(count, PAIR_DEV, SAMPLES), pos_second.reshape(count, PAIR_DEV, SAMPLES))

def reference(first_scene, second_scene, rad_first, rad_second, pos_first, pos_second, prior_weight):
    width = 2 * BANDS * TERMS
    blocks = blocked(first_scene, second_scene, rad_first, rad_second, pos_first, pos_second)

    def start_step(acc, blk):
        fidx, sidx, ra, rb, qa, qb = blk
        la = ra.astype(jnp.float32)
        lb = rb.astype(jnp.float32)
        pa = legendre(qa)
        pb = legendre(qb)
        mismatch = la - lb
        term_a = jnp.concatenate([-pull(mismatch, la, pa).reshape(PAIR_DEV, width), diag_terms(la, pa).reshape(PAIR_DEV, width)], axis=1)
        term_b = jnp.concatenate([pull(mismatch, lb, pb).reshape(PAIR_DEV, width), diag_terms(lb, pb).reshape(PAIR_DEV, width)], axis=1)
        acc = acc + jax.ops.segment_sum(term_a, fidx, num_segments=SCENES) + jax.ops.segment_sum(term_b, sidx, num_segments=SCENES)
        return (acc, None)
    acc, _ = lax.scan(start_step, jnp.zeros((SCENES, 2 * width), jnp.float32), blocks)
    rhs = acc[:, :width]
    jacobi = acc[:, width:] + prior_weight[:, None]

    def operate(direction):
        coef = direction.reshape(SCENES, 2, BANDS, TERMS)

        def step(total, blk):
            fidx, sidx, ra, rb, qa, qb = blk
            la = ra.astype(jnp.float32)
            lb = rb.astype(jnp.float32)
            pa = legendre(qa)
            pb = legendre(qb)
            resid = predict(coef[fidx], la, pa) - predict(coef[sidx], lb, pb)
            ga = pull(resid, la, pa).reshape(PAIR_DEV, width)
            gb = -pull(resid, lb, pb).reshape(PAIR_DEV, width)
            total = total + jax.ops.segment_sum(ga, fidx, num_segments=SCENES) + jax.ops.segment_sum(gb, sidx, num_segments=SCENES)
            return (total, None)
        total, _ = lax.scan(step, jnp.zeros((SCENES, width), jnp.float32), blocks)
        return total + prior_weight[:, None] * direction
    solution = jnp.zeros((SCENES, width), jnp.float32)
    residual = rhs
    precond = residual / jacobi
    direction = precond
    norm_now = jnp.sum(residual * precond)
    for step_index in range(ITERS):
        image = operate(direction)
        alpha = norm_now / jnp.sum(direction * image)
        solution = solution + alpha * direction
        residual = residual - alpha * image
        precond = residual / jacobi
        norm_next = jnp.sum(residual * precond)
        direction = precond + norm_next / norm_now * direction
        norm_now = norm_next
    return (solution, residual)
```

```python
import functools
import math

import jax
import jax.numpy as jnp
from jax import lax
from jax.experimental import pallas as pl
from jax.experimental.pallas import tpu as pltpu
from jax.sharding import PartitionSpec as P

TERMS = 64
COLS = 1024
LANES = 128
OWNED = 8
UNROLL = 4
MESH = pl.DeviceIdType.MESH
F32 = jnp.float32
BF16 = jnp.bfloat16


def row_chunks(bands):
    return ((0, bands // 2), (bands // 2, bands // 2))


def groups_of(n):
    return ((8, 1), (4, 8), (4, 32)) if n == 128 else ((n, 1),)


def split(x):
    hi = x.astype(BF16)
    lo = (x - hi.astype(F32)).astype(BF16)
    return hi, lo


def halves(x):
    hi, lo = split(x)
    return jnp.concatenate([hi, lo], axis=1)


def low_lanes(rows):
    return lax.broadcasted_iota(jnp.int32, (rows, LANES), 1) < TERMS


def swap(x):
    return pltpu.roll(x, TERMS, 1)


def fold(x):
    return jnp.sum(x.reshape(x.shape[0] // 8, 8, LANES), axis=0)


def kernel(
    n,
    fs_ref, ss_ref, pw_ref, ra_ref, rb_ref, qa_ref, qb_ref,
    out_s, out_r,
    leg_a, leg_b, wj_a, wj_b, wt, w2_a, w2_b,
    run, run_d, run_o, coef,
    own0, ahead0, recv_l0, recv_r0,
    own1, ahead1, recv_l1, recv_r1,
    own2, ahead2, recv_l2,
    tile_l, tile_r, recv_tl, recv_tr,
    res, zz, inv, az, ww, diag_o, prior, macc,
    red_src, red_dst,
    slot, prev, last,
    sem_s0, sem_r0, sem_s1, sem_r1, sem_s2, sem_r2, sem_t, red_ssem, red_rsem,
):
    me = lax.axis_index("scene")
    right, left = lax.rem(me + 1, n), lax.rem(me + n - 1, n)
    pairs, bands = ra_ref.shape[0], ra_ref.shape[1]
    halfs = 2 * pairs
    chunks = row_chunks(bands)
    groups = groups_of(n)
    peers = []
    for size, stride in groups:
        place = (me // stride) % size
        for j in range(1, size):
            peers.append((me - place * stride) + ((place + j) % size) * stride)

    barrier = pltpu.get_barrier_semaphore()
    for other in [left, right] + peers:
        pl.semaphore_signal(barrier, inc=1, device_id=(other,), device_id_type=MESH)

    for i in range(2 * OWNED):
        last[i] = halfs

    def link(p, carry):
        a = fs_ref[p] - me * OWNED
        b = ss_ref[p] - me * OWNED
        b = jnp.where(b < 0, b + n * OWNED, b)
        for h, scene in ((2 * p, a), (2 * p + 1, b)):
            scene = jnp.clip(scene, 0, 2 * OWNED - 1)
            slot[h] = scene
            before = jnp.int32(halfs)
            after = []
            for i in range(2 * OWNED):
                hit = scene == i
                before = jnp.where(hit, carry[i], before)
                after.append(jnp.where(hit, h, carry[i]))
            prev[h] = before
            carry = tuple(after)
        return carry

    ends = lax.fori_loop(0, pairs, link, tuple(jnp.int32(halfs) for _ in range(2 * OWNED)))
    for i in range(2 * OWNED):
        last[i] = ends[i]

    for q_ref, leg in ((qa_ref, leg_a), (qb_ref, leg_b)):
        sign = 1.0 if leg is leg_a else -1.0
        t = q_ref[...].astype(F32) * (2.0 / (COLS - 1)) - 1.0
        before, now = jnp.ones_like(t), t
        for k in range(TERMS):
            leg[pl.ds(k * pairs, pairs), :] = before * (sign * 0.0625 * math.sqrt(2 * k + 1))
            before, now = now, ((2 * k + 3) / (k + 2)) * t * now - ((k + 1) / (k + 2)) * before

    run[halfs] = jnp.zeros(run.shape[1:], F32)
    run_d[halfs] = jnp.zeros(run_d.shape[1:], F32)
    run_o[halfs] = jnp.zeros(run_o.shape[1:], F32)
    macc[...] = jnp.zeros(macc.shape, F32)

    def weights(p, _):
        tops = []
        for side, (leg, wj, w2) in enumerate(((leg_a, wj_a, w2_a), (leg_b, wj_b, w2_b))):
            phi = leg[pl.ds(p, TERMS, stride=pairs), :]
            hi, lo = split(phi)
            wj[p] = jnp.concatenate([hi, lo, hi, lo], axis=0)
            top = jnp.concatenate([hi.astype(F32), lo.astype(F32)], axis=0)
            tops.append(top.T.astype(BF16))
            square = phi * phi
            hi, lo = split(square)
            top = jnp.concatenate([hi.astype(F32), lo.astype(F32)], axis=0)
            turned = top.T.astype(BF16)
            w2[p] = turned
            sums = jnp.dot(jnp.ones((16, LANES), BF16), turned, preferred_element_type=F32)
            h = 2 * p + side
            run_o[h] = sums[:8] + run_o[prev[h]]
        wt[p] = jnp.concatenate(tops, axis=1)
        return 0

    lax.fori_loop(0, pairs, weights, 0)

    for s in range(2 * OWNED):
        total = run_o[last[s]]
        total = total + swap(total)
        tile = tile_l if s < OWNED else tile_r
        row = s % OWNED
        tile[pl.ds(row, 1), :] = total[:1]
    for s in range(OWNED):
        tile_l[pl.ds(OWNED + s, 1), :] = jnp.full((1, LANES), pw_ref[s], F32)

    pl.semaphore_wait(barrier, 2 + len(peers))
    tiles = [
        pltpu.make_async_remote_copy(tile_r, recv_tl, sem_t.at[0], sem_t.at[1], device_id=(right,), device_id_type=MESH),
        pltpu.make_async_remote_copy(tile_l, recv_tr, sem_t.at[2], sem_t.at[3], device_id=(left,), device_id_type=MESH),
    ]
    for copy in tiles:
        copy.start()

    def transfers(c, rows, to_right, to_left, send, recv):
        r0, size = rows
        moves = []
        for way, (pair, other) in enumerate(((to_right, right), (to_left, left))):
            if pair is not None:
                src, dst = pair
                moves.append(
                    pltpu.make_async_remote_copy(
                        src.at[:, pl.ds(r0, size), :],
                        dst.at[:, pl.ds(r0, size), :],
                        send.at[2 * c + way],
                        recv.at[2 * c + way],
                        device_id=(other,),
                        device_id_type=MESH,
                    )
                )
        return moves

    def pull(p, size, e, la, lb):
        weight = wt[p]
        weight = jnp.concatenate([weight, weight], axis=0)
        both = jnp.dot(halves(e), weight, preferred_element_type=F32)
        gain_a = jnp.dot(halves(la * e), weight[:, :LANES], preferred_element_type=F32)
        gain_b = jnp.dot(halves(lb * e), weight[:, LANES:], preferred_element_type=F32)
        low = low_lanes(size)
        for side, gain in ((0, gain_a), (1, gain_b)):
            offset = both[:, side * LANES : (side + 1) * LANES]
            term = jnp.where(low, gain, offset) + swap(jnp.where(low, offset, gain))
            h = 2 * p + side
            run[h, :size, :] = term + run[prev[h], :size, :]

    def over_pairs(body, init):
        def step(g, carry):
            for u in range(UNROLL):
                carry = body(g * UNROLL + u, carry)
            return carry

        return lax.fori_loop(0, pairs // UNROLL, step, init)

    moves0 = []
    for c, (r0, size) in enumerate(chunks):
        rows = pl.ds(r0, size)

        def start_pair(p, carry):
            la = ra_ref[p, rows, :].astype(F32)
            lb = rb_ref[p, rows, :].astype(F32)
            pull(p, size, lb - la, la, lb)
            for side, (rad, w2) in enumerate(((la, w2_a), (lb, w2_b))):
                weight = w2[p]
                weight = jnp.concatenate([weight, weight], axis=0)
                h = 2 * p + side
                term = jnp.dot(halves(rad * rad), weight, preferred_element_type=F32)
                run_d[h, :size, :] = term + run_d[prev[h], :size, :]
            return carry

        over_pairs(start_pair, 0)
        low = low_lanes(size)
        for base, buf in ((0, own0), (OWNED, ahead0)):
            for s in range(OWNED):
                buf[s, rows, :] = run[last[base + s], :size, :]
            for s in range(OWNED // 2):
                one = run_d[last[base + s], :size, :]
                two = run_d[last[base + s + OWNED // 2], :size, :]
                buf[OWNED + s, rows, :] = jnp.where(low, one, two) + swap(jnp.where(low, two, one))
        moves = transfers(c, (r0, size), (ahead0, recv_l0), (own0, recv_r0), sem_s0, sem_r0)
        for copy in moves:
            copy.start()
        moves0.append(moves)

    def spread(s, size, z):
        low = low_lanes(size)
        turned = swap(z)
        coef[s, 0, :size, :] = halves(jnp.where(low, z, turned))
        coef[s, 1, :size, :] = halves(jnp.where(low, turned, z))

    def apply_pair(rows, size, index):
        def body(p, total):
            la = ra_ref[p, rows, :].astype(F32)
            lb = rb_ref[p, rows, :].astype(F32)
            fields = []
            for side, wj in ((0, wj_a), (1, wj_b)):
                both = coef[slot[2 * p + side]]
                weight = wj[p]
                for part in range(2):
                    fields.append(jnp.dot(both[part, :size, :], weight, preferred_element_type=F32))
            e = (la * fields[0] + fields[1]) + (lb * fields[2] + fields[3])
            pull(p, size, e, la, lb)
            return total + fold(e * e)

        macc[index] += over_pairs(body, jnp.zeros((8, LANES), F32))

    for copy in tiles:
        copy.wait()
    diag_o[pl.ds(0, OWNED), :] = tile_l[pl.ds(0, OWNED), :] + recv_tl[...]
    diag_o[pl.ds(OWNED, OWNED), :] = tile_r[...] + recv_tr[pl.ds(0, OWNED), :]
    prior[pl.ds(0, OWNED), :] = tile_l[pl.ds(OWNED, OWNED), :]
    prior[pl.ds(OWNED, OWNED), :] = recv_tr[pl.ds(OWNED, OWNED), :]

    moves1 = []
    for c, (r0, size) in enumerate(chunks):
        rows = pl.ds(r0, size)
        for copy in moves0[c]:
            copy.wait()
        low = low_lanes(size)
        for base, mine, theirs in ((0, own0, recv_l0), (OWNED, ahead0, recv_r0)):
            for half in range(2):
                for i in range(OWNED // 2):
                    row = half * (OWNED // 2) + i
                    s = base + row
                    gain = mine[OWNED + i, rows, :] + theirs[OWNED + i, rows, :]
                    if half:
                        gain = swap(gain)
                    weight = prior[pl.ds(s, 1), :]
                    jacobi = jnp.where(low, gain, diag_o[pl.ds(s, 1), :]) + weight
                    inverse = 1.0 / jacobi
                    r = mine[row, rows, :] + theirs[row, rows, :]
                    z = r * inverse
                    inv[s, rows, :] = inverse
                    zz[s, rows, :] = z
                    if base == 0:
                        res[s, rows, :] = r
                        macc[0] += fold(r * z)
                        macc[1] += fold(weight * (z * z))
                    spread(s, size, z)
        apply_pair(rows, size, 1)
        for base, buf in ((0, own1), (OWNED, ahead1)):
            for s in range(OWNED):
                buf[s, rows, :] = run[last[base + s], :size, :]
        moves = transfers(c, (r0, size), (ahead1, recv_l1), (own1, recv_r1), sem_s1, sem_r1)
        for copy in moves:
            copy.start()
        moves1.append(moves)

    moves2 = []
    for c, (r0, size) in enumerate(chunks):
        rows = pl.ds(r0, size)
        for copy in moves1[c]:
            copy.wait()
        for base, mine, theirs in ((0, own1, recv_l1), (OWNED, ahead1, recv_r1)):
            for row in range(OWNED):
                s = base + row
                weight = prior[pl.ds(s, 1), :]
                image = mine[row, rows, :] + theirs[row, rows, :] + weight * zz[s, rows, :]
                w = image * inv[s, rows, :]
                if base == 0:
                    az[s, rows, :] = image
                    ww[s, rows, :] = w
                    macc[2] += fold(image * w)
                    macc[3] += fold(weight * (w * w))
                spread(s, size, w)
        apply_pair(rows, size, 3)
        for base, buf in ((0, own2), (OWNED, ahead2)):
            for s in range(OWNED):
                buf[s, rows, :] = run[last[base + s], :size, :]
        moves = transfers(c, (r0, size), (ahead2, recv_l2), None, sem_s2, sem_r2)
        for copy in moves:
            copy.start()
        moves2.append(moves)

    sums = [jnp.sum(macc[i], axis=0, keepdims=True) for i in range(4)]
    tile = jnp.concatenate(sums + [jnp.zeros((4, LANES), F32)], axis=0)
    count = 0
    for g, (size, stride) in enumerate(groups):
        red_src[g] = tile
        copies = []
        for j in range(1, size):
            copies.append(
                pltpu.make_async_remote_copy(
                    red_src.at[g], red_dst.at[count], red_ssem.at[count], red_rsem.at[count],
                    device_id=(peers[count],), device_id_type=MESH,
                )
            )
            copies[-1].start()
            count += 1
        for j, copy in enumerate(copies):
            copy.wait()
            tile = tile + red_dst[count - len(copies) + j]
    tile = jnp.sum(tile, axis=1, keepdims=True)
    m0, m1, m2, m3 = (tile[i : i + 1, :] for i in range(4))
    first = m0 / m1
    ratio = first * m2 / m1
    again = (ratio - 1.0) * m0
    second = again / (ratio * (ratio * m1 - 2.0 * first * m2) + first * first * m3)
    of_z = first + second * ratio
    of_w = -second * first

    for c, (r0, size) in enumerate(chunks):
        for copy in moves2[c]:
            copy.wait()
        half = size // 2
        low = low_lanes(half)
        for s in range(OWNED):
            weight = prior[pl.ds(s, 1), :]
            parts = []
            for odd in range(2):
                rows = pl.ds(r0 + odd, half, stride=2)
                w = ww[s, rows, :]
                last_image = own2[s, rows, :] + recv_l2[s, rows, :] + weight * w
                parts.append(
                    (
                        of_z * zz[s, rows, :] + of_w * w,
                        res[s, rows, :] - of_z * az[s, rows, :] - of_w * last_image,
                    )
                )
            for out, even, odd in ((out_s, parts[0][0], parts[1][0]), (out_r, parts[0][1], parts[1][1])):
                out[pl.ds((r0 // 2) * OWNED + s, half, stride=OWNED), :] = jnp.where(low, even, swap(odd))
                out[pl.ds((bands // 2 + r0 // 2) * OWNED + s, half, stride=OWNED), :] = jnp.where(low, swap(even), odd)


def shards(n, first_scene, second_scene, rad_first, rad_second, pos_first, pos_second, prior_weight):
    pairs, bands = rad_first.shape[:2]
    halfs = 2 * pairs
    chunks = row_chunks(bands)
    most = max(size for _, size in chunks)
    peers = sum(size - 1 for size, _ in groups_of(n))
    smem = pl.BlockSpec(memory_space=pltpu.SMEM)
    vmem = pl.BlockSpec(memory_space=pltpu.VMEM)

    def block(rows):
        return pltpu.VMEM((rows, bands, LANES), F32)

    flat = jax.ShapeDtypeStruct((bands * OWNED, LANES), F32)
    outs = pl.pallas_call(
        functools.partial(kernel, n),
        out_shape=(flat, flat),
        in_specs=[smem, smem, smem, vmem, vmem, vmem, vmem],
        out_specs=(vmem, vmem),
        scratch_shapes=[
            pltpu.VMEM((TERMS * pairs, LANES), F32),
            pltpu.VMEM((TERMS * pairs, LANES), F32),
            pltpu.VMEM((pairs, 4 * TERMS, LANES), BF16),
            pltpu.VMEM((pairs, 4 * TERMS, LANES), BF16),
            pltpu.VMEM((pairs, LANES, 2 * LANES), BF16),
            pltpu.VMEM((pairs, LANES, LANES), BF16),
            pltpu.VMEM((pairs, LANES, LANES), BF16),
            pltpu.VMEM((halfs + 1, most, LANES), F32),
            pltpu.VMEM((halfs + 1, most, LANES), F32),
            pltpu.VMEM((halfs + 1, 8, LANES), F32),
            pltpu.VMEM((2 * OWNED, 2, most, 2 * LANES), BF16),
            block(12), block(12), block(12), block(12),
            block(8), block(8), block(8), block(8),
            block(8), block(8), block(8),
            pltpu.VMEM((2 * OWNED, LANES), F32),
            pltpu.VMEM((OWNED, LANES), F32),
            pltpu.VMEM((OWNED, LANES), F32),
            pltpu.VMEM((2 * OWNED, LANES), F32),
            block(8), block(16), block(16), block(8), block(8),
            pltpu.VMEM((2 * OWNED, LANES), F32),
            pltpu.VMEM((2 * OWNED, LANES), F32),
            pltpu.VMEM((4, 8, LANES), F32),
            pltpu.VMEM((len(groups_of(n)), 8, LANES), F32),
            pltpu.VMEM((peers, 8, LANES), F32),
            pltpu.SMEM((halfs,), jnp.int32),
            pltpu.SMEM((halfs,), jnp.int32),
            pltpu.SMEM((2 * OWNED,), jnp.int32),
            pltpu.SemaphoreType.DMA((2 * len(chunks),)),
            pltpu.SemaphoreType.DMA((2 * len(chunks),)),
            pltpu.SemaphoreType.DMA((2 * len(chunks),)),
            pltpu.SemaphoreType.DMA((2 * len(chunks),)),
            pltpu.SemaphoreType.DMA((2 * len(chunks),)),
            pltpu.SemaphoreType.DMA((2 * len(chunks),)),
            pltpu.SemaphoreType.DMA((4,)),
            pltpu.SemaphoreType.DMA((peers,)),
            pltpu.SemaphoreType.DMA((peers,)),
        ],
        compiler_params=pltpu.CompilerParams(
            collective_id=0, has_side_effects=True, vmem_limit_bytes=56 * 1024 * 1024
        ),
    )(first_scene, second_scene, prior_weight, rad_first, rad_second, pos_first, pos_second)
    return tuple(
        x.reshape(bands, OWNED, LANES).transpose(1, 0, 2).reshape(OWNED, bands * LANES) for x in outs
    )


def solution(mesh):
    return jax.shard_map(
        functools.partial(shards, mesh.shape["scene"]),
        mesh=mesh,
        in_specs=(
            P("scene"),
            P("scene"),
            P("scene", None, None),
            P("scene", None, None),
            P("scene", None),
            P("scene", None),
            P("scene"),
        ),
        out_specs=(P("scene", None), P("scene", None)),
        check_vma=False,
    )
```

```python
import functools
import math

import jax
import jax.numpy as jnp
from jax import lax
from jax.experimental import pallas as pl
from jax.experimental.pallas import tpu as pltpu
from jax.sharding import PartitionSpec as P

TERMS = 64
COLS = 1024
LANES = 128
OWNED = 8
UNROLL = 8
PREPARE = 4
MESH = pl.DeviceIdType.MESH
F32 = jnp.float32
BF16 = jnp.bfloat16


def row_chunks(bands):
    sizes = (64, 80, 80) if bands == 224 else (bands // 2, bands - bands // 2)
    chunks, start = [], 0
    for size in sizes:
        chunks.append((start, size))
        start += size
    return chunks


def groups_of(n):
    return ((8, 1), (4, 8), (4, 32)) if n == 128 else ((n, 1),)


def split(x):
    hi = x.astype(BF16)
    lo = (x - hi.astype(F32)).astype(BF16)
    return hi, lo


def halves(x):
    hi, lo = split(x)
    return jnp.concatenate([hi, lo], axis=1)


def low_lanes(rows):
    return lax.broadcasted_iota(jnp.int32, (rows, LANES), 1) < TERMS


def swap(x):
    return pltpu.roll(x, TERMS, 1)


def fold(x):
    return jnp.sum(x.reshape(x.shape[0] // 8, 8, LANES), axis=0)


def kernel(
    n,
    fs_ref, ss_ref, pw_ref, ra_hbm, rb_hbm, qa_ref, qb_ref,
    out_s, out_r,
    ra_ref, rb_ref, leg_a, leg_b, wj, wt, w2,
    run, run_d, run_o, coef,
    own0, ahead0, recv_l0, recv_r0,
    own1, ahead1, recv_l1, recv_r1,
    own2, ahead2, recv_l2,
    tile_l, tile_r, recv_tl, recv_tr,
    res, zz, inv, az, ww, diag_o, prior, macc,
    red_src, red_dst,
    slot, prev, last,
    sem_s0, sem_r0, sem_s1, sem_r1, sem_s2, sem_r2, sem_t, sem_in, red_ssem, red_rsem,
):
    me = lax.axis_index("scene")
    right, left = lax.rem(me + 1, n), lax.rem(me + n - 1, n)
    pairs, bands = ra_ref.shape[0], ra_ref.shape[1]
    halfs = 2 * pairs
    chunks = row_chunks(bands)
    groups = groups_of(n)
    peers = []
    for size, stride in groups:
        place = (me // stride) % size
        for j in range(1, size):
            peers.append((me - place * stride) + ((place + j) % size) * stride)

    loads = [
        pltpu.make_async_copy(ra_hbm, ra_ref, sem_in.at[0]),
        pltpu.make_async_copy(rb_hbm, rb_ref, sem_in.at[1]),
    ]
    for load in loads:
        load.start()

    barrier = pltpu.get_barrier_semaphore()
    for other in [left, right] + peers:
        pl.semaphore_signal(barrier, inc=1, device_id=(other,), device_id_type=MESH)

    for q_ref, leg in ((qa_ref, leg_a), (qb_ref, leg_b)):
        sign = 1.0 if leg is leg_a else -1.0
        t = q_ref[...].astype(F32) * (2.0 / (COLS - 1)) - 1.0
        before, now = jnp.ones_like(t), t
        for k in range(TERMS):
            leg[pl.ds(k * pairs, pairs), :] = before * (sign * 0.0625 * math.sqrt(2 * k + 1))
            before, now = now, ((2 * k + 3) / (k + 2)) * t * now - ((k + 1) / (k + 2)) * before

    run[halfs] = jnp.zeros(run.shape[1:], F32)
    run_d[halfs] = jnp.zeros(run_d.shape[1:], F32)
    run_o[halfs] = jnp.zeros(run_o.shape[1:], F32)
    macc[...] = jnp.zeros(macc.shape, F32)

    def link(p, ends):
        a = fs_ref[p] - me * OWNED
        b = ss_ref[p] - me * OWNED
        b = jnp.where(b < 0, b + n * OWNED, b)
        for h, scene in ((2 * p, a), (2 * p + 1, b)):
            scene = jnp.clip(scene, 0, 2 * OWNED - 1)
            slot[h] = scene
            before = jnp.int32(halfs)
            after = []
            for i in range(2 * OWNED):
                hit = scene == i
                before = jnp.where(hit, ends[i], before)
                after.append(jnp.where(hit, h, ends[i]))
            prev[h] = before
            ends = tuple(after)
        return ends

    def weights(p):
        low = low_lanes(LANES)
        his, los, turned, squares = [], [], [], []
        for leg in (leg_a, leg_b):
            hi, lo = split(leg[pl.ds(p, TERMS, stride=pairs), :])
            his.append(hi)
            los.append(lo)
            wide = jnp.concatenate([hi.astype(F32), lo.astype(F32)], axis=0).T
            turned.append(wide.astype(BF16))
            phi = wide + swap(wide)
            hi, lo = split(phi * phi)
            squares.append(jnp.where(low, hi, lo))
        wj[p] = jnp.concatenate([jnp.concatenate(his, axis=1), jnp.concatenate(los, axis=1)], axis=0)
        wt[p] = jnp.concatenate(turned, axis=1)
        square = jnp.concatenate(squares, axis=1)
        w2[p] = square
        sums = jnp.dot(jnp.ones((16, LANES), BF16), square, preferred_element_type=F32)
        for side in range(2):
            h = 2 * p + side
            run_o[h] = sums[:8, side * LANES : (side + 1) * LANES] + run_o[prev[h]]

    def prepare(g, ends):
        for u in range(PREPARE):
            ends = link(g * PREPARE + u, ends)
        for u in range(PREPARE):
            weights(g * PREPARE + u)
        return ends

    ends = lax.fori_loop(0, pairs // PREPARE, prepare, tuple(jnp.int32(halfs) for _ in range(2 * OWNED)))
    for i in range(2 * OWNED):
        last[i] = ends[i]

    for s in range(2 * OWNED):
        total = run_o[last[s]]
        total = total + swap(total)
        tile = tile_l if s < OWNED else tile_r
        row = s % OWNED
        tile[pl.ds(row, 1), :] = total[:1]
    for s in range(OWNED):
        tile_l[pl.ds(OWNED + s, 1), :] = jnp.full((1, LANES), pw_ref[s], F32)

    pl.semaphore_wait(barrier, 2 + len(peers))
    tiles = [
        pltpu.make_async_remote_copy(tile_r, recv_tl, sem_t.at[0], sem_t.at[1], device_id=(right,), device_id_type=MESH),
        pltpu.make_async_remote_copy(tile_l, recv_tr, sem_t.at[2], sem_t.at[3], device_id=(left,), device_id_type=MESH),
    ]
    for copy in tiles:
        copy.start()

    def transfers(c, rows, to_right, to_left, send, recv):
        r0, size = rows
        moves = []
        for way, (pair, other) in enumerate(((to_right, right), (to_left, left))):
            if pair is not None:
                src, dst = pair
                moves.append(
                    pltpu.make_async_remote_copy(
                        src.at[:, pl.ds(r0, size), :],
                        dst.at[:, pl.ds(r0, size), :],
                        send.at[2 * c + way],
                        recv.at[2 * c + way],
                        device_id=(other,),
                        device_id_type=MESH,
                    )
                )
        return moves

    def twice(x):
        return jnp.concatenate([x, x], axis=0)

    def pull(p, size, e, la, lb):
        left_side = jnp.concatenate([halves(e), halves(la * e), halves(lb * e)], axis=0)
        terms = jnp.dot(left_side, twice(wt[p]), preferred_element_type=F32)
        for side in range(2):
            lanes = slice(side * LANES, (side + 1) * LANES)
            h = 2 * p + side
            before = prev[h]
            run[h, 0, :size, :] = terms[(1 + side) * size : (2 + side) * size, lanes] + run[before, 0, :size, :]
            run[h, 1, :size, :] = terms[:size, lanes] + run[before, 1, :size, :]

    def scene_total(s, size):
        low = low_lanes(size)
        gain, offset = run[last[s], 0, :size, :], run[last[s], 1, :size, :]
        return jnp.where(low, gain, offset) + swap(jnp.where(low, offset, gain))

    def over_pairs(body, init):
        def step(g, carry):
            for u in range(UNROLL):
                carry = body(g * UNROLL + u, carry)
            return carry

        return lax.fori_loop(0, pairs // UNROLL, step, init)

    for load in loads:
        load.wait()
    moves0 = []
    for c, (r0, size) in enumerate(chunks):
        rows = pl.ds(r0, size)

        def start_pair(p, carry):
            la = ra_ref[p, rows, :].astype(F32)
            lb = rb_ref[p, rows, :].astype(F32)
            pull(p, size, lb - la, la, lb)
            squares = jnp.concatenate([halves(la * la), halves(lb * lb)], axis=0)
            terms = jnp.dot(squares, twice(w2[p]), preferred_element_type=F32)
            for side in range(2):
                h = 2 * p + side
                run_d[h, :size, :] = (
                    terms[side * size : (side + 1) * size, side * LANES : (side + 1) * LANES]
                    + run_d[prev[h], :size, :]
                )
            return carry

        over_pairs(start_pair, 0)
        low = low_lanes(size)
        for base, buf in ((0, own0), (OWNED, ahead0)):
            for s in range(OWNED):
                buf[s, rows, :] = scene_total(base + s, size)
            for s in range(OWNED // 2):
                one = run_d[last[base + s], :size, :]
                two = run_d[last[base + s + OWNED // 2], :size, :]
                buf[OWNED + s, rows, :] = jnp.where(low, one, two) + swap(jnp.where(low, two, one))
        moves = transfers(c, (r0, size), (ahead0, recv_l0), (own0, recv_r0), sem_s0, sem_r0)
        for copy in moves:
            copy.start()
        moves0.append(moves)

    def spread(s, size, z):
        low = low_lanes(size)
        turned = swap(z)
        hi, lo = split(z)
        hi_turned, lo_turned = split(turned)
        coef[s, 0, :size, :] = jnp.where(low, hi, lo_turned)
        coef[s, 1, :size, :] = jnp.where(low, hi_turned, lo)

    nought = jnp.zeros((LANES, LANES), BF16)

    def apply_pairs(rows, size, index):
        def product(p):
            la = ra_ref[p, rows, :].astype(F32)
            lb = rb_ref[p, rows, :].astype(F32)
            one, two = coef[slot[2 * p]], coef[slot[2 * p + 1]]
            left_side = jnp.concatenate(
                [
                    jnp.concatenate([one[0, :size, :], one[1, :size, :]], axis=0),
                    jnp.concatenate([two[0, :size, :], two[1, :size, :]], axis=0),
                ],
                axis=1,
            )
            left_side = jnp.concatenate([left_side, left_side], axis=1)
            parts = []
            for part in range(2):
                weight = twice(wj[p, part * TERMS : (part + 1) * TERMS, :])
                parts.append(jnp.concatenate([weight[:, :LANES], nought], axis=1))
                parts.append(jnp.concatenate([nought, weight[:, LANES:]], axis=1))
            fields = jnp.dot(left_side, jnp.concatenate(parts, axis=0), preferred_element_type=F32)
            gain_a, offset_a = fields[:size, :LANES], fields[size:, :LANES]
            gain_b, offset_b = fields[:size, LANES:], fields[size:, LANES:]
            return (la * gain_a + lb * gain_b) + (offset_a + offset_b)

        def rest(p, e, total):
            la = ra_ref[p, rows, :].astype(F32)
            lb = rb_ref[p, rows, :].astype(F32)
            pull(p, size, e, la, lb)
            return total + fold(e * e)

        def step(g, total):
            e = product(g * UNROLL)
            for u in range(UNROLL):
                after = product(g * UNROLL + u + 1) if u + 1 < UNROLL else None
                total = rest(g * UNROLL + u, e, total)
                e = after
            return total

        macc[index] += lax.fori_loop(0, pairs // UNROLL, step, jnp.zeros((8, LANES), F32))

    for copy in tiles:
        copy.wait()
    diag_o[pl.ds(0, OWNED), :] = tile_l[pl.ds(0, OWNED), :] + recv_tl[...]
    diag_o[pl.ds(OWNED, OWNED), :] = tile_r[...] + recv_tr[pl.ds(0, OWNED), :]
    prior[pl.ds(0, OWNED), :] = tile_l[pl.ds(OWNED, OWNED), :]
    prior[pl.ds(OWNED, OWNED), :] = recv_tr[pl.ds(OWNED, OWNED), :]

    moves1 = []
    for c, (r0, size) in enumerate(chunks):
        rows = pl.ds(r0, size)
        for copy in moves0[c]:
            copy.wait()
        low = low_lanes(size)
        for base, mine, theirs in ((0, own0, recv_l0), (OWNED, ahead0, recv_r0)):
            for half in range(2):
                for i in range(OWNED // 2):
                    row = half * (OWNED // 2) + i
                    s = base + row
                    gain = mine[OWNED + i, rows, :] + theirs[OWNED + i, rows, :]
                    if half:
                        gain = swap(gain)
                    weight = prior[pl.ds(s, 1), :]
                    jacobi = jnp.where(low, gain, diag_o[pl.ds(s, 1), :]) + weight
                    inverse = 1.0 / jacobi
                    r = mine[row, rows, :] + theirs[row, rows, :]
                    z = r * inverse
                    inv[s, rows, :] = inverse
                    zz[s, rows, :] = z
                    if base == 0:
                        res[s, rows, :] = r
                        macc[0] += fold(r * z)
                        macc[1] += fold(weight * (z * z))
                    spread(s, size, z)
        apply_pairs(rows, size, 1)
        for base, buf in ((0, own1), (OWNED, ahead1)):
            for s in range(OWNED):
                buf[s, rows, :] = scene_total(base + s, size)
        moves = transfers(c, (r0, size), (ahead1, recv_l1), (own1, recv_r1), sem_s1, sem_r1)
        for copy in moves:
            copy.start()
        moves1.append(moves)

    moves2 = []
    for c, (r0, size) in enumerate(chunks):
        rows = pl.ds(r0, size)
        for copy in moves1[c]:
            copy.wait()
        for base, mine, theirs in ((0, own1, recv_l1), (OWNED, ahead1, recv_r1)):
            for row in range(OWNED):
                s = base + row
                weight = prior[pl.ds(s, 1), :]
                image = mine[row, rows, :] + theirs[row, rows, :] + weight * zz[s, rows, :]
                w = image * inv[s, rows, :]
                if base == 0:
                    az[s, rows, :] = image
                    ww[s, rows, :] = w
                    macc[2] += fold(image * w)
                    macc[3] += fold(weight * (w * w))
                spread(s, size, w)
        apply_pairs(rows, size, 3)
        for base, buf in ((0, own2), (OWNED, ahead2)):
            for s in range(OWNED):
                buf[s, rows, :] = scene_total(base + s, size)
        moves = transfers(c, (r0, size), (ahead2, recv_l2), None, sem_s2, sem_r2)
        if c < len(chunks) - 1:
            for copy in moves:
                copy.start()
        moves2.append(moves)

    sums = [jnp.sum(macc[i], axis=0, keepdims=True) for i in range(4)]
    tile = jnp.concatenate(sums + [jnp.zeros((4, LANES), F32)], axis=0)
    count = 0
    for g, (size, stride) in enumerate(groups):
        red_src[g] = tile
        copies = []
        for j in range(1, size):
            copies.append(
                pltpu.make_async_remote_copy(
                    red_src.at[g], red_dst.at[count], red_ssem.at[count], red_rsem.at[count],
                    device_id=(peers[count],), device_id_type=MESH,
                )
            )
            copies[-1].start()
            count += 1
        if g == 0:
            for copy in moves2[-1]:
                copy.start()
        for j, copy in enumerate(copies):
            copy.wait()
            tile = tile + red_dst[count - len(copies) + j]
    tile = jnp.sum(tile, axis=1, keepdims=True)
    m0, m1, m2, m3 = (tile[i : i + 1, :] for i in range(4))
    first = m0 / m1
    ratio = first * m2 / m1
    again = (ratio - 1.0) * m0
    second = again / (ratio * (ratio * m1 - 2.0 * first * m2) + first * first * m3)
    of_z = first + second * ratio
    of_w = -second * first

    for c, (r0, size) in enumerate(chunks):
        for copy in moves2[c]:
            copy.wait()
        half = size // 2
        low = low_lanes(half)
        for s in range(OWNED):
            weight = prior[pl.ds(s, 1), :]
            parts = []
            for odd in range(2):
                rows = pl.ds(r0 + odd, half, stride=2)
                w = ww[s, rows, :]
                last_image = own2[s, rows, :] + recv_l2[s, rows, :] + weight * w
                parts.append(
                    (
                        of_z * zz[s, rows, :] + of_w * w,
                        res[s, rows, :] - of_z * az[s, rows, :] - of_w * last_image,
                    )
                )
            for out, even, odd in ((out_s, parts[0][0], parts[1][0]), (out_r, parts[0][1], parts[1][1])):
                out[pl.ds((r0 // 2) * OWNED + s, half, stride=OWNED), :] = jnp.where(low, even, swap(odd))
                out[pl.ds((bands // 2 + r0 // 2) * OWNED + s, half, stride=OWNED), :] = jnp.where(low, swap(even), odd)


def shards(n, first_scene, second_scene, rad_first, rad_second, pos_first, pos_second, prior_weight):
    pairs, bands = rad_first.shape[:2]
    halfs = 2 * pairs
    chunks = row_chunks(bands)
    most = max(size for _, size in chunks)
    peers = sum(size - 1 for size, _ in groups_of(n))
    smem = pl.BlockSpec(memory_space=pltpu.SMEM)
    vmem = pl.BlockSpec(memory_space=pltpu.VMEM)
    hbm = pl.BlockSpec(memory_space=pl.ANY)

    def block(rows):
        return pltpu.VMEM((rows, bands, LANES), F32)

    flat = jax.ShapeDtypeStruct((bands * OWNED, LANES), F32)
    outs = pl.pallas_call(
        functools.partial(kernel, n),
        out_shape=(pltpu.VMEM(flat.shape, F32), pltpu.VMEM(flat.shape, F32)),
        in_specs=[smem, smem, smem, hbm, hbm, vmem, vmem],
        out_specs=(vmem, vmem),
        scratch_shapes=[
            pltpu.VMEM((pairs, bands, LANES), BF16),
            pltpu.VMEM((pairs, bands, LANES), BF16),
            pltpu.VMEM((TERMS * pairs, LANES), F32),
            pltpu.VMEM((TERMS * pairs, LANES), F32),
            pltpu.VMEM((pairs, 2 * TERMS, 2 * LANES), BF16),
            pltpu.VMEM((pairs, LANES, 2 * LANES), BF16),
            pltpu.VMEM((pairs, LANES, 2 * LANES), BF16),
            pltpu.VMEM((halfs + 1, 2, most, LANES), F32),
            pltpu.VMEM((halfs + 1, most, LANES), F32),
            pltpu.VMEM((halfs + 1, 8, LANES), F32),
            pltpu.VMEM((2 * OWNED, 2, most, LANES), BF16),
            block(12), block(12), block(12), block(12),
            block(8), block(8), block(8), block(8),
            block(8), block(8), block(8),
            pltpu.VMEM((2 * OWNED, LANES), F32),
            pltpu.VMEM((OWNED, LANES), F32),
            pltpu.VMEM((OWNED, LANES), F32),
            pltpu.VMEM((2 * OWNED, LANES), F32),
            block(8), block(16), block(16), block(8), block(8),
            pltpu.VMEM((2 * OWNED, LANES), F32),
            pltpu.VMEM((2 * OWNED, LANES), F32),
            pltpu.VMEM((4, 8, LANES), F32),
            pltpu.VMEM((len(groups_of(n)), 8, LANES), F32),
            pltpu.VMEM((peers, 8, LANES), F32),
            pltpu.SMEM((halfs,), jnp.int32),
            pltpu.SMEM((halfs,), jnp.int32),
            pltpu.SMEM((2 * OWNED,), jnp.int32),
            pltpu.SemaphoreType.DMA((2 * len(chunks),)),
            pltpu.SemaphoreType.DMA((2 * len(chunks),)),
            pltpu.SemaphoreType.DMA((2 * len(chunks),)),
            pltpu.SemaphoreType.DMA((2 * len(chunks),)),
            pltpu.SemaphoreType.DMA((2 * len(chunks),)),
            pltpu.SemaphoreType.DMA((2 * len(chunks),)),
            pltpu.SemaphoreType.DMA((4,)),
            pltpu.SemaphoreType.DMA((2,)),
            pltpu.SemaphoreType.DMA((peers,)),
            pltpu.SemaphoreType.DMA((peers,)),
        ],
        compiler_params=pltpu.CompilerParams(
            collective_id=0, has_side_effects=True, vmem_limit_bytes=56 * 1024 * 1024
        ),
    )(first_scene, second_scene, prior_weight, rad_first, rad_second, pos_first, pos_second)
    return tuple(
        x.reshape(bands, OWNED, LANES).transpose(1, 0, 2).reshape(OWNED, bands * LANES) for x in outs
    )


def solution(mesh):
    return jax.shard_map(
        functools.partial(shards, mesh.shape["scene"]),
        mesh=mesh,
        in_specs=(
            P("scene"),
            P("scene"),
            P("scene", None, None),
            P("scene", None, None),
            P("scene", None),
            P("scene", None),
            P("scene"),
        ),
        out_specs=(P("scene", None), P("scene", None)),
        check_vma=False,
    )
```

```python
import functools
import math

import jax
import jax.numpy as jnp
from jax import lax
from jax.experimental import pallas as pl
from jax.experimental.pallas import tpu as pltpu
from jax.sharding import PartitionSpec as P

TERMS = 64
COLS = 1024
LANES = 128
OWNED = 8
UNROLL = 12
PREPARE = 4
MESH = pl.DeviceIdType.MESH
F32 = jnp.float32
BF16 = jnp.bfloat16


def row_chunks(bands):
    sizes = (64, 80, 80) if bands == 224 else (bands // 2, bands - bands // 2)
    chunks, start = [], 0
    for size in sizes:
        chunks.append((start, size))
        start += size
    return chunks


def groups_of(n):
    return ((16, 1), (8, 16)) if n == 128 else ((n, 1),)


def split(x):
    hi = x.astype(BF16)
    lo = (x - hi.astype(F32)).astype(BF16)
    return hi, lo


def halves(x):
    hi, lo = split(x)
    return jnp.concatenate([hi, lo], axis=1)


def against(x, rows):
    return lax.dot_general(x, rows, (((1,), (1,)), ((), ())), preferred_element_type=F32)


def beside(x):
    return jnp.concatenate([x, x], axis=1)


def low_lanes(rows):
    return lax.broadcasted_iota(jnp.int32, (rows, LANES), 1) < TERMS


def swap(x):
    return pltpu.roll(x, TERMS, 1)


def fold(x):
    return jnp.sum(x.reshape(x.shape[0] // 8, 8, LANES), axis=0)


def kernel(
    n,
    fs_ref, ss_ref, pw_ref, ra_hbm, rb_hbm, qa_ref, qb_ref,
    out_s, out_r,
    ra_ref, rb_ref, leg_a, leg_b, wj, wt, w2,
    run, run_d, run_o, coef, held,
    own0, ahead0, recv_l0, recv_r0,
    own1, ahead1, recv_l1, recv_r1,
    own2, ahead2, recv_l2,
    tile_l, tile_r, recv_tl, recv_tr,
    res, zz, inv, az, ww, diag_o, prior, macc,
    red_src, red_dst,
    slot, prev, last,
    sem_s0, sem_r0, sem_s1, sem_r1, sem_s2, sem_r2, sem_t, sem_in, red_ssem, red_rsem,
):
    me = lax.axis_index("scene")
    right, left = lax.rem(me + 1, n), lax.rem(me + n - 1, n)
    pairs, bands = ra_ref.shape[0], ra_ref.shape[1]
    halfs = 2 * pairs
    chunks = row_chunks(bands)
    groups = groups_of(n)
    peers = []
    for size, stride in groups:
        place = (me // stride) % size
        for j in range(1, size):
            peers.append((me - place * stride) + ((place + j) % size) * stride)

    loads = [
        pltpu.make_async_copy(ra_hbm, ra_ref, sem_in.at[0]),
        pltpu.make_async_copy(rb_hbm, rb_ref, sem_in.at[1]),
    ]
    for load in loads:
        load.start()

    barrier = pltpu.get_barrier_semaphore()
    for other in [left, right] + peers:
        pl.semaphore_signal(barrier, inc=1, device_id=(other,), device_id_type=MESH)

    for q_ref, leg in ((qa_ref, leg_a), (qb_ref, leg_b)):
        sign = 1.0 if leg is leg_a else -1.0
        t = q_ref[...].astype(F32) * (2.0 / (COLS - 1)) - 1.0
        before, now = jnp.ones_like(t), t
        for k in range(TERMS):
            leg[pl.ds(k * pairs, pairs), :] = before * (sign * 0.0625 * math.sqrt(2 * k + 1))
            before, now = now, ((2 * k + 3) / (k + 2)) * t * now - ((k + 1) / (k + 2)) * before

    run[halfs] = jnp.zeros(run.shape[1:], F32)
    run_d[halfs] = jnp.zeros(run_d.shape[1:], F32)
    run_o[halfs] = jnp.zeros(run_o.shape[1:], F32)
    macc[...] = jnp.zeros(macc.shape, F32)

    def link(p, ends):
        a = fs_ref[p] - me * OWNED
        b = ss_ref[p] - me * OWNED
        b = jnp.where(b < 0, b + n * OWNED, b)
        for h, scene in ((2 * p, a), (2 * p + 1, b)):
            scene = jnp.clip(scene, 0, 2 * OWNED - 1)
            slot[h] = scene
            before = jnp.int32(halfs)
            after = []
            for i in range(2 * OWNED):
                hit = scene == i
                before = jnp.where(hit, ends[i], before)
                after.append(jnp.where(hit, h, ends[i]))
            prev[h] = before
            ends = tuple(after)
        return ends

    def weights(p):
        his, los, rows, squares = [], [], [], []
        for leg in (leg_a, leg_b):
            phi = leg[pl.ds(p, TERMS, stride=pairs), :]
            hi, lo = split(phi)
            his.append(hi)
            los.append(lo)
            rows += [hi, lo]
            squares += list(split(phi * phi))
        wj[p] = jnp.concatenate([jnp.concatenate(his, axis=1), jnp.concatenate(los, axis=1)], axis=0)
        wt[p] = jnp.concatenate(rows, axis=0)
        square = jnp.concatenate(squares, axis=0)
        w2[p] = square
        sums = against(jnp.ones((16, LANES), BF16), square)
        for side in range(2):
            h = 2 * p + side
            run_o[h] = sums[:8, side * LANES : (side + 1) * LANES] + run_o[prev[h]]

    def prepare(g, ends):
        for u in range(PREPARE):
            ends = link(g * PREPARE + u, ends)
        for u in range(PREPARE):
            weights(g * PREPARE + u)
        return ends

    ends = lax.fori_loop(0, pairs // PREPARE, prepare, tuple(jnp.int32(halfs) for _ in range(2 * OWNED)))
    for i in range(2 * OWNED):
        last[i] = ends[i]

    for s in range(2 * OWNED):
        total = run_o[last[s]]
        total = total + swap(total)
        tile = tile_l if s < OWNED else tile_r
        row = s % OWNED
        tile[pl.ds(row, 1), :] = total[:1]
    for s in range(OWNED):
        tile_l[pl.ds(OWNED + s, 1), :] = jnp.full((1, LANES), pw_ref[s], F32)

    pl.semaphore_wait(barrier, 2 + len(peers))
    tiles = [
        pltpu.make_async_remote_copy(tile_r, recv_tl, sem_t.at[0], sem_t.at[1], device_id=(right,), device_id_type=MESH),
        pltpu.make_async_remote_copy(tile_l, recv_tr, sem_t.at[2], sem_t.at[3], device_id=(left,), device_id_type=MESH),
    ]
    for copy in tiles:
        copy.start()

    def transfers(c, rows, to_right, to_left, send, recv):
        r0, size = rows
        moves = []
        for way, (pair, other) in enumerate(((to_right, right), (to_left, left))):
            if pair is not None:
                src, dst = pair
                moves.append(
                    pltpu.make_async_remote_copy(
                        src.at[:, pl.ds(r0, size), :],
                        dst.at[:, pl.ds(r0, size), :],
                        send.at[2 * c + way],
                        recv.at[2 * c + way],
                        device_id=(other,),
                        device_id_type=MESH,
                    )
                )
        return moves

    def twice(x):
        return jnp.concatenate([x, x], axis=0)

    def pull(p, size, e, la, lb):
        left_side = jnp.concatenate([halves(e), halves(la * e), halves(lb * e)], axis=0)
        terms = against(left_side, beside(wt[p]))
        for side in range(2):
            lanes = slice(side * LANES, (side + 1) * LANES)
            h = 2 * p + side
            before = prev[h]
            run[h, 0, :size, :] = terms[(1 + side) * size : (2 + side) * size, lanes] + run[before, 0, :size, :]
            run[h, 1, :size, :] = terms[:size, lanes] + run[before, 1, :size, :]

    def scene_total(s, size):
        low = low_lanes(size)
        gain, offset = run[last[s], 0, :size, :], run[last[s], 1, :size, :]
        return jnp.where(low, gain, offset) + swap(jnp.where(low, offset, gain))

    def over_pairs(body, init):
        def step(g, carry):
            for u in range(UNROLL):
                carry = body(g * UNROLL + u, carry)
            return carry

        return lax.fori_loop(0, pairs // UNROLL, step, init)

    for load in loads:
        load.wait()
    moves0 = []
    for c, (r0, size) in enumerate(chunks):
        rows = pl.ds(r0, size)

        def start_pair(p, carry):
            la = ra_ref[p, rows, :].astype(F32)
            lb = rb_ref[p, rows, :].astype(F32)
            pull(p, size, lb - la, la, lb)
            squares = jnp.concatenate([halves(la * la), halves(lb * lb)], axis=0)
            terms = against(squares, beside(w2[p]))
            for side in range(2):
                h = 2 * p + side
                run_d[h, :size, :] = (
                    terms[side * size : (side + 1) * size, side * LANES : (side + 1) * LANES]
                    + run_d[prev[h], :size, :]
                )
            return carry

        over_pairs(start_pair, 0)
        low = low_lanes(size)
        for base, buf in ((0, own0), (OWNED, ahead0)):
            for s in range(OWNED):
                buf[s, rows, :] = scene_total(base + s, size)
            for s in range(OWNED // 2):
                one = run_d[last[base + s], :size, :]
                two = run_d[last[base + s + OWNED // 2], :size, :]
                buf[OWNED + s, rows, :] = jnp.where(low, one, two) + swap(jnp.where(low, two, one))
        moves = transfers(c, (r0, size), (ahead0, recv_l0), (own0, recv_r0), sem_s0, sem_r0)
        for copy in moves:
            copy.start()
        moves0.append(moves)

    def spread(s, size, z):
        low = low_lanes(size)
        turned = swap(z)
        hi, lo = split(z)
        hi_turned, lo_turned = split(turned)
        coef[s, 0, :size, :] = jnp.where(low, hi, lo_turned)
        coef[s, 1, :size, :] = jnp.where(low, hi_turned, lo)

    nought = jnp.zeros((LANES, LANES), BF16)

    def apply_pairs(rows, size, index, between=None):
        def product(p):
            la = ra_ref[p, rows, :].astype(F32)
            lb = rb_ref[p, rows, :].astype(F32)
            one, two = coef[slot[2 * p]], coef[slot[2 * p + 1]]
            left_side = jnp.concatenate([one[0, :size, :], one[1, :size, :], two[0, :size, :], two[1, :size, :]], axis=0)
            left_side = jnp.concatenate([left_side, left_side], axis=1)
            weight = jnp.concatenate([twice(wj[p, :TERMS, :]), twice(wj[p, TERMS:, :])], axis=0)
            fields = jnp.dot(left_side, weight, preferred_element_type=F32)
            gain_a, offset_a = fields[:size, :LANES], fields[size : 2 * size, :LANES]
            gain_b, offset_b = fields[2 * size : 3 * size, LANES:], fields[3 * size :, LANES:]
            return (la * gain_a + lb * gain_b) + (offset_a + offset_b)

        def rest(p, e, total):
            la = ra_ref[p, rows, :].astype(F32)
            lb = rb_ref[p, rows, :].astype(F32)
            pull(p, size, e, la, lb)
            return total + fold(e * e)

        def step(g, total):
            e = product(g * UNROLL)
            for u in range(UNROLL):
                after = product(g * UNROLL + u + 1) if u + 1 < UNROLL else None
                total = rest(g * UNROLL + u, e, total)
                e = after
            return total

        def products(g, total):
            for u in range(UNROLL):
                p = g * UNROLL + u
                e = product(p)
                held[p, :size, :] = e
                total = total + fold(e * e)
            return total

        def pulls(g, carry):
            for u in range(UNROLL):
                p = g * UNROLL + u
                la = ra_ref[p, rows, :].astype(F32)
                lb = rb_ref[p, rows, :].astype(F32)
                pull(p, size, held[p, :size, :], la, lb)
            return carry

        nothing = jnp.zeros((8, LANES), F32)
        if between is None:
            macc[index] += lax.fori_loop(0, pairs // UNROLL, step, nothing)
        else:
            macc[index] += lax.fori_loop(0, pairs // UNROLL, products, nothing)
            between()
            lax.fori_loop(0, pairs // UNROLL, pulls, 0)

    for copy in tiles:
        copy.wait()
    diag_o[pl.ds(0, OWNED), :] = tile_l[pl.ds(0, OWNED), :] + recv_tl[...]
    diag_o[pl.ds(OWNED, OWNED), :] = tile_r[...] + recv_tr[pl.ds(0, OWNED), :]
    prior[pl.ds(0, OWNED), :] = tile_l[pl.ds(OWNED, OWNED), :]
    prior[pl.ds(OWNED, OWNED), :] = recv_tr[pl.ds(OWNED, OWNED), :]

    moves1 = []
    for c, (r0, size) in enumerate(chunks):
        rows = pl.ds(r0, size)
        for copy in moves0[c]:
            copy.wait()
        low = low_lanes(size)
        for base, mine, theirs in ((0, own0, recv_l0), (OWNED, ahead0, recv_r0)):
            for half in range(2):
                for i in range(OWNED // 2):
                    row = half * (OWNED // 2) + i
                    s = base + row
                    gain = mine[OWNED + i, rows, :] + theirs[OWNED + i, rows, :]
                    if half:
                        gain = swap(gain)
                    weight = prior[pl.ds(s, 1), :]
                    jacobi = jnp.where(low, gain, diag_o[pl.ds(s, 1), :]) + weight
                    inverse = 1.0 / jacobi
                    r = mine[row, rows, :] + theirs[row, rows, :]
                    z = r * inverse
                    inv[s, rows, :] = inverse
                    zz[s, rows, :] = z
                    if base == 0:
                        res[s, rows, :] = r
                        macc[0] += fold(r * z)
                        macc[1] += fold(weight * (z * z))
                    spread(s, size, z)
        apply_pairs(rows, size, 1)
        for base, buf in ((0, own1), (OWNED, ahead1)):
            for s in range(OWNED):
                buf[s, rows, :] = scene_total(base + s, size)
        moves = transfers(c, (r0, size), (ahead1, recv_l1), (own1, recv_r1), sem_s1, sem_r1)
        for copy in moves:
            copy.start()
        moves1.append(moves)

    rounds = []

    def send_sums(g, tile):
        red_src[g] = tile
        first_peer = sum(size - 1 for size, _ in groups[:g])
        copies = []
        for count in range(first_peer, first_peer + groups[g][0] - 1):
            copy = pltpu.make_async_remote_copy(
                red_src.at[g], red_dst.at[count], red_ssem.at[count], red_rsem.at[count],
                device_id=(peers[count],), device_id_type=MESH,
            )
            copy.start()
            copies.append((count, copy))
        rounds.append(copies)

    def start_sums():
        sums = [jnp.sum(macc[i], axis=0, keepdims=True) for i in range(4)]
        send_sums(0, jnp.concatenate(sums + [jnp.zeros((4, LANES), F32)], axis=0))

    moves2 = []
    for c, (r0, size) in enumerate(chunks):
        rows = pl.ds(r0, size)
        for copy in moves1[c]:
            copy.wait()
        for base, mine, theirs in ((0, own1, recv_l1), (OWNED, ahead1, recv_r1)):
            for row in range(OWNED):
                s = base + row
                weight = prior[pl.ds(s, 1), :]
                image = mine[row, rows, :] + theirs[row, rows, :] + weight * zz[s, rows, :]
                w = image * inv[s, rows, :]
                if base == 0:
                    az[s, rows, :] = image
                    ww[s, rows, :] = w
                    macc[2] += fold(image * w)
                    macc[3] += fold(weight * (w * w))
                spread(s, size, w)
        apply_pairs(rows, size, 3, start_sums if c == len(chunks) - 1 else None)
        for base, buf in ((0, own2), (OWNED, ahead2)):
            for s in range(OWNED):
                buf[s, rows, :] = scene_total(base + s, size)
        moves = transfers(c, (r0, size), (ahead2, recv_l2), None, sem_s2, sem_r2)
        for copy in moves:
            copy.start()
        moves2.append(moves)

    for g in range(len(groups)):
        if g > 0:
            send_sums(g, tile)
        tile = red_src[g]
        for count, copy in rounds[g]:
            copy.wait()
            tile = tile + red_dst[count]
    tile = jnp.sum(tile, axis=1, keepdims=True)
    m0, m1, m2, m3 = (tile[i : i + 1, :] for i in range(4))
    first = m0 / m1
    ratio = first * m2 / m1
    again = (ratio - 1.0) * m0
    second = again / (ratio * (ratio * m1 - 2.0 * first * m2) + first * first * m3)
    of_z = first + second * ratio
    of_w = -second * first

    for c, (r0, size) in enumerate(chunks):
        for copy in moves2[c]:
            copy.wait()
        half = size // 2
        low = low_lanes(half)
        for s in range(OWNED):
            weight = prior[pl.ds(s, 1), :]
            parts = []
            for odd in range(2):
                rows = pl.ds(r0 + odd, half, stride=2)
                w = ww[s, rows, :]
                last_image = own2[s, rows, :] + recv_l2[s, rows, :] + weight * w
                parts.append(
                    (
                        of_z * zz[s, rows, :] + of_w * w,
                        res[s, rows, :] - of_z * az[s, rows, :] - of_w * last_image,
                    )
                )
            for out, even, odd in ((out_s, parts[0][0], parts[1][0]), (out_r, parts[0][1], parts[1][1])):
                out[pl.ds((r0 // 2) * OWNED + s, half, stride=OWNED), :] = jnp.where(low, even, swap(odd))
                out[pl.ds((bands // 2 + r0 // 2) * OWNED + s, half, stride=OWNED), :] = jnp.where(low, swap(even), odd)


def shards(n, first_scene, second_scene, rad_first, rad_second, pos_first, pos_second, prior_weight):
    pairs, bands = rad_first.shape[:2]
    halfs = 2 * pairs
    chunks = row_chunks(bands)
    most = max(size for _, size in chunks)
    peers = sum(size - 1 for size, _ in groups_of(n))
    smem = pl.BlockSpec(memory_space=pltpu.SMEM)
    vmem = pl.BlockSpec(memory_space=pltpu.VMEM)
    hbm = pl.BlockSpec(memory_space=pl.ANY)

    def block(rows):
        return pltpu.VMEM((rows, bands, LANES), F32)

    flat = jax.ShapeDtypeStruct((bands * OWNED, LANES), F32)
    outs = pl.pallas_call(
        functools.partial(kernel, n),
        out_shape=(pltpu.VMEM(flat.shape, F32), pltpu.VMEM(flat.shape, F32)),
        in_specs=[smem, smem, smem, hbm, hbm, vmem, vmem],
        out_specs=(vmem, vmem),
        scratch_shapes=[
            pltpu.VMEM((pairs, bands, LANES), BF16),
            pltpu.VMEM((pairs, bands, LANES), BF16),
            pltpu.VMEM((TERMS * pairs, LANES), F32),
            pltpu.VMEM((TERMS * pairs, LANES), F32),
            pltpu.VMEM((pairs, 2 * TERMS, 2 * LANES), BF16),
            pltpu.VMEM((pairs, 4 * TERMS, LANES), BF16),
            pltpu.VMEM((pairs, 4 * TERMS, LANES), BF16),
            pltpu.VMEM((halfs + 1, 2, most, LANES), F32),
            pltpu.VMEM((halfs + 1, most, LANES), F32),
            pltpu.VMEM((halfs + 1, 8, LANES), F32),
            pltpu.VMEM((2 * OWNED, 2, most, LANES), BF16),
            pltpu.VMEM((pairs, most, LANES), F32),
            block(12), block(12), block(12), block(12),
            block(8), block(8), block(8), block(8),
            block(8), block(8), block(8),
            pltpu.VMEM((2 * OWNED, LANES), F32),
            pltpu.VMEM((OWNED, LANES), F32),
            pltpu.VMEM((OWNED, LANES), F32),
            pltpu.VMEM((2 * OWNED, LANES), F32),
            block(8), block(16), block(16), block(8), block(8),
            pltpu.VMEM((2 * OWNED, LANES), F32),
            pltpu.VMEM((2 * OWNED, LANES), F32),
            pltpu.VMEM((4, 8, LANES), F32),
            pltpu.VMEM((len(groups_of(n)), 8, LANES), F32),
            pltpu.VMEM((peers, 8, LANES), F32),
            pltpu.SMEM((halfs,), jnp.int32),
            pltpu.SMEM((halfs,), jnp.int32),
            pltpu.SMEM((2 * OWNED,), jnp.int32),
            pltpu.SemaphoreType.DMA((2 * len(chunks),)),
            pltpu.SemaphoreType.DMA((2 * len(chunks),)),
            pltpu.SemaphoreType.DMA((2 * len(chunks),)),
            pltpu.SemaphoreType.DMA((2 * len(chunks),)),
            pltpu.SemaphoreType.DMA((2 * len(chunks),)),
            pltpu.SemaphoreType.DMA((2 * len(chunks),)),
            pltpu.SemaphoreType.DMA((4,)),
            pltpu.SemaphoreType.DMA((2,)),
            pltpu.SemaphoreType.DMA((peers,)),
            pltpu.SemaphoreType.DMA((peers,)),
        ],
        compiler_params=pltpu.CompilerParams(
            collective_id=0, has_side_effects=True, vmem_limit_bytes=56 * 1024 * 1024
        ),
    )(first_scene, second_scene, prior_weight, rad_first, rad_second, pos_first, pos_second)
    return tuple(
        x.reshape(bands, OWNED, LANES).transpose(1, 0, 2).reshape(OWNED, bands * LANES) for x in outs
    )


def solution(mesh):
    return jax.shard_map(
        functools.partial(shards, mesh.shape["scene"]),
        mesh=mesh,
        in_specs=(
            P("scene"),
            P("scene"),
            P("scene", None, None),
            P("scene", None, None),
            P("scene", None),
            P("scene", None),
            P("scene"),
        ),
        out_specs=(P("scene", None), P("scene", None)),
        check_vma=False,
    )
```

```python
import functools
import math

import jax
import jax.numpy as jnp
from jax import lax
from jax.experimental import pallas as pl
from jax.experimental.pallas import tpu as pltpu
from jax.sharding import PartitionSpec as P

TERMS = 64
COLS = 1024
LANES = 128
OWNED = 8
UNROLL = 12
PREPARE = 4
MESH = pl.DeviceIdType.MESH
F32 = jnp.float32
BF16 = jnp.bfloat16


def row_chunks(bands):
    sizes = (64, 80, 80) if bands == 224 else (bands // 2, bands - bands // 2)
    chunks, start = [], 0
    for size in sizes:
        chunks.append((start, size))
        start += size
    return chunks


def groups_of(n):
    return ((16, 1), (8, 16)) if n == 128 else ((n, 1),)


def split(x):
    hi = x.astype(BF16)
    lo = (x - hi.astype(F32)).astype(BF16)
    return hi, lo


def halves(x):
    hi, lo = split(x)
    return jnp.concatenate([hi, lo], axis=1)


def against(x, rows):
    return lax.dot_general(x, rows, (((1,), (1,)), ((), ())), preferred_element_type=F32)


def beside(x):
    return jnp.concatenate([x, x], axis=1)


def low_lanes(rows):
    return lax.broadcasted_iota(jnp.int32, (rows, LANES), 1) < TERMS


def swap(x):
    return pltpu.roll(x, TERMS, 1)


def fold(x):
    return jnp.sum(x.reshape(x.shape[0] // 8, 8, LANES), axis=0)


def kernel(
    n,
    fs_ref, ss_ref, pw_ref, ra_hbm, rb_hbm, qa_ref, qb_ref,
    out_s, out_r,
    ra_ref, rb_ref, leg_a, leg_b, wj, wt, w2,
    run, run_d, run_o, coef, held,
    own0, ahead0, recv_l0, recv_r0,
    own1, ahead1, recv_l1, recv_r1,
    own2, ahead2, recv_l2,
    tile_l, tile_r, recv_tl, recv_tr,
    res, zz, inv, az, ww, diag_o, prior, macc,
    red_src, red_dst,
    slot, prev, last,
    sem_s0, sem_r0, sem_s1, sem_r1, sem_s2, sem_r2, sem_t, sem_in, red_ssem, red_rsem,
):
    me = lax.axis_index("scene")
    right, left = lax.rem(me + 1, n), lax.rem(me + n - 1, n)
    pairs, bands = ra_ref.shape[0], ra_ref.shape[1]
    halfs = 2 * pairs
    chunks = row_chunks(bands)
    groups = groups_of(n)
    peers = []
    for size, stride in groups:
        place = (me // stride) % size
        for j in range(1, size):
            peers.append((me - place * stride) + ((place + j) % size) * stride)

    loads = [
        pltpu.make_async_copy(ra_hbm, ra_ref, sem_in.at[0]),
        pltpu.make_async_copy(rb_hbm, rb_ref, sem_in.at[1]),
    ]
    for load in loads:
        load.start()

    barrier = pltpu.get_barrier_semaphore()
    for other in [left, right] + peers:
        pl.semaphore_signal(barrier, inc=1, device_id=(other,), device_id_type=MESH)

    for q_ref, leg in ((qa_ref, leg_a), (qb_ref, leg_b)):
        sign = 1.0 if leg is leg_a else -1.0
        t = q_ref[...].astype(F32) * (2.0 / (COLS - 1)) - 1.0
        before, now = jnp.ones_like(t), t
        for k in range(TERMS):
            leg[pl.ds(k * pairs, pairs), :] = before * (sign * 0.0625 * math.sqrt(2 * k + 1))
            before, now = now, ((2 * k + 3) / (k + 2)) * t * now - ((k + 1) / (k + 2)) * before

    run[halfs] = jnp.zeros(run.shape[1:], F32)
    run_d[halfs] = jnp.zeros(run_d.shape[1:], F32)
    run_o[halfs] = jnp.zeros(run_o.shape[1:], F32)
    macc[...] = jnp.zeros(macc.shape, F32)

    def link(p, ends):
        a = fs_ref[p] - me * OWNED
        b = ss_ref[p] - me * OWNED
        b = jnp.where(b < 0, b + n * OWNED, b)
        for h, scene in ((2 * p, a), (2 * p + 1, b)):
            scene = jnp.clip(scene, 0, 2 * OWNED - 1)
            slot[h] = scene
            before = jnp.int32(halfs)
            after = []
            for i in range(2 * OWNED):
                hit = scene == i
                before = jnp.where(hit, ends[i], before)
                after.append(jnp.where(hit, h, ends[i]))
            prev[h] = before
            ends = tuple(after)
        return ends

    def weights(p):
        his, los, rows, squares = [], [], [], []
        for leg in (leg_a, leg_b):
            phi = leg[pl.ds(p, TERMS, stride=pairs), :]
            hi, lo = split(phi)
            his.append(hi)
            los.append(lo)
            rows += [hi, lo]
            squares += list(split(phi * phi))
        wj[p] = jnp.concatenate([jnp.concatenate(his, axis=1), jnp.concatenate(los, axis=1)], axis=0)
        wt[p] = jnp.concatenate(rows, axis=0)
        square = jnp.concatenate(squares, axis=0)
        w2[p] = square
        sums = against(jnp.ones((16, LANES), BF16), square)
        for side in range(2):
            h = 2 * p + side
            run_o[h] = sums[:8, side * LANES : (side + 1) * LANES] + run_o[prev[h]]

    def prepare(g, ends):
        for u in range(PREPARE):
            ends = link(g * PREPARE + u, ends)
        for u in range(PREPARE):
            weights(g * PREPARE + u)
        return ends

    ends = lax.fori_loop(0, pairs // PREPARE, prepare, tuple(jnp.int32(halfs) for _ in range(2 * OWNED)))
    for i in range(2 * OWNED):
        last[i] = ends[i]

    for s in range(2 * OWNED):
        total = run_o[last[s]]
        total = total + swap(total)
        tile = tile_l if s < OWNED else tile_r
        row = s % OWNED
        tile[pl.ds(row, 1), :] = total[:1]
    for s in range(OWNED):
        tile_l[pl.ds(OWNED + s, 1), :] = jnp.full((1, LANES), pw_ref[s], F32)

    pl.semaphore_wait(barrier, 2 + len(peers))
    tiles = [
        pltpu.make_async_remote_copy(tile_r, recv_tl, sem_t.at[0], sem_t.at[1], device_id=(right,), device_id_type=MESH),
        pltpu.make_async_remote_copy(tile_l, recv_tr, sem_t.at[2], sem_t.at[3], device_id=(left,), device_id_type=MESH),
    ]
    for copy in tiles:
        copy.start()

    def transfers(c, rows, to_right, to_left, send, recv):
        r0, size = rows
        moves = []
        for way, (pair, other) in enumerate(((to_right, right), (to_left, left))):
            if pair is not None:
                src, dst = pair
                moves.append(
                    pltpu.make_async_remote_copy(
                        src.at[:, pl.ds(r0, size), :],
                        dst.at[:, pl.ds(r0, size), :],
                        send.at[2 * c + way],
                        recv.at[2 * c + way],
                        device_id=(other,),
                        device_id_type=MESH,
                    )
                )
        return moves

    def twice(x):
        return jnp.concatenate([x, x], axis=0)

    def pull(p, size, e, la, lb):
        left_side = jnp.concatenate([halves(e), halves(la * e), halves(lb * e)], axis=0)
        terms = against(left_side, beside(wt[p]))
        for side in range(2):
            lanes = slice(side * LANES, (side + 1) * LANES)
            h = 2 * p + side
            before = prev[h]
            run[h, 0, :size, :] = terms[(1 + side) * size : (2 + side) * size, lanes] + run[before, 0, :size, :]
            run[h, 1, :size, :] = terms[:size, lanes] + run[before, 1, :size, :]

    def scene_total(s, size):
        low = low_lanes(size)
        gain, offset = run[last[s], 0, :size, :], run[last[s], 1, :size, :]
        return jnp.where(low, gain, offset) + swap(jnp.where(low, offset, gain))

    def over_pairs(body, init):
        def step(g, carry):
            for u in range(UNROLL):
                carry = body(g * UNROLL + u, carry)
            return carry

        return lax.fori_loop(0, pairs // UNROLL, step, init)

    for load in loads:
        load.wait()
    moves0 = []
    for c, (r0, size) in enumerate(chunks):
        rows = pl.ds(r0, size)

        def start_pair(p, carry):
            la = ra_ref[p, rows, :].astype(F32)
            lb = rb_ref[p, rows, :].astype(F32)
            pull(p, size, lb - la, la, lb)
            squares = jnp.concatenate([halves(la * la), halves(lb * lb)], axis=0)
            terms = against(squares, beside(w2[p]))
            for side in range(2):
                h = 2 * p + side
                run_d[h, :size, :] = (
                    terms[side * size : (side + 1) * size, side * LANES : (side + 1) * LANES]
                    + run_d[prev[h], :size, :]
                )
            return carry

        over_pairs(start_pair, 0)
        low = low_lanes(size)
        for base, buf in ((0, own0), (OWNED, ahead0)):
            for s in range(OWNED):
                buf[s, rows, :] = scene_total(base + s, size)
            for s in range(OWNED // 2):
                one = run_d[last[base + s], :size, :]
                two = run_d[last[base + s + OWNED // 2], :size, :]
                buf[OWNED + s, rows, :] = jnp.where(low, one, two) + swap(jnp.where(low, two, one))
        moves = transfers(c, (r0, size), (ahead0, recv_l0), (own0, recv_r0), sem_s0, sem_r0)
        for copy in moves:
            copy.start()
        moves0.append(moves)

    def spread(s, size, z):
        low = low_lanes(size)
        turned = swap(z)
        hi, lo = split(z)
        hi_turned, lo_turned = split(turned)
        coef[s, 0, :size, :] = jnp.where(low, hi, lo_turned)
        coef[s, 1, :size, :] = jnp.where(low, hi_turned, lo)

    nought = jnp.zeros((LANES, LANES), BF16)

    def apply_pairs(rows, size, index, between=None):
        def product(p):
            la = ra_ref[p, rows, :].astype(F32)
            lb = rb_ref[p, rows, :].astype(F32)
            one, two = coef[slot[2 * p]], coef[slot[2 * p + 1]]
            left_side = jnp.concatenate([one[0, :size, :], one[1, :size, :], two[0, :size, :], two[1, :size, :]], axis=0)
            left_side = jnp.concatenate([left_side, left_side], axis=1)
            weight = jnp.concatenate([twice(wj[p, :TERMS, :]), twice(wj[p, TERMS:, :])], axis=0)
            fields = jnp.dot(left_side, weight, preferred_element_type=F32)
            gain_a, offset_a = fields[:size, :LANES], fields[size : 2 * size, :LANES]
            gain_b, offset_b = fields[2 * size : 3 * size, LANES:], fields[3 * size :, LANES:]
            return (la * gain_a + lb * gain_b) + (offset_a + offset_b)

        def rest(p, e, total):
            la = ra_ref[p, rows, :].astype(F32)
            lb = rb_ref[p, rows, :].astype(F32)
            pull(p, size, e, la, lb)
            return total + fold(e * e)

        def step(g, total):
            e = product(g * UNROLL)
            for u in range(UNROLL):
                after = product(g * UNROLL + u + 1) if u + 1 < UNROLL else None
                total = rest(g * UNROLL + u, e, total)
                e = after
            return total

        def products(g, total):
            for u in range(UNROLL):
                p = g * UNROLL + u
                e = product(p)
                held[p, :size, :] = e
                total = total + fold(e * e)
            return total

        def pulls(g, carry):
            for u in range(UNROLL):
                p = g * UNROLL + u
                la = ra_ref[p, rows, :].astype(F32)
                lb = rb_ref[p, rows, :].astype(F32)
                pull(p, size, held[p, :size, :], la, lb)
            return carry

        nothing = jnp.zeros((8, LANES), F32)
        if between is None:
            macc[index] += lax.fori_loop(0, pairs // UNROLL, step, nothing)
        else:
            macc[index] += lax.fori_loop(0, pairs // UNROLL, products, nothing)
            between()
            lax.fori_loop(0, pairs // UNROLL, pulls, 0)

    for copy in tiles:
        copy.wait()
    diag_o[pl.ds(0, OWNED), :] = tile_l[pl.ds(0, OWNED), :] + recv_tl[...]
    diag_o[pl.ds(OWNED, OWNED), :] = tile_r[...] + recv_tr[pl.ds(0, OWNED), :]
    prior[pl.ds(0, OWNED), :] = tile_l[pl.ds(OWNED, OWNED), :]
    prior[pl.ds(OWNED, OWNED), :] = recv_tr[pl.ds(OWNED, OWNED), :]

    moves1 = []
    for c, (r0, size) in enumerate(chunks):
        rows = pl.ds(r0, size)
        for copy in moves0[c]:
            copy.wait_recv()
        low = low_lanes(size)
        for base, mine, theirs in ((0, own0, recv_l0), (OWNED, ahead0, recv_r0)):
            for half in range(2):
                for i in range(OWNED // 2):
                    row = half * (OWNED // 2) + i
                    s = base + row
                    gain = mine[OWNED + i, rows, :] + theirs[OWNED + i, rows, :]
                    if half:
                        gain = swap(gain)
                    weight = prior[pl.ds(s, 1), :]
                    jacobi = jnp.where(low, gain, diag_o[pl.ds(s, 1), :]) + weight
                    inverse = 1.0 / jacobi
                    r = mine[row, rows, :] + theirs[row, rows, :]
                    z = r * inverse
                    inv[s, rows, :] = inverse
                    zz[s, rows, :] = z
                    if base == 0:
                        res[s, rows, :] = r
                        macc[0] += fold(r * z)
                        macc[1] += fold(weight * (z * z))
                    spread(s, size, z)
        apply_pairs(rows, size, 1)
        for base, buf in ((0, own1), (OWNED, ahead1)):
            for s in range(OWNED):
                buf[s, rows, :] = scene_total(base + s, size)
        moves = transfers(c, (r0, size), (ahead1, recv_l1), (own1, recv_r1), sem_s1, sem_r1)
        for copy in moves:
            copy.start()
        moves1.append(moves)

    rounds = []

    def send_sums(g, tile):
        red_src[g] = tile
        first_peer = sum(size - 1 for size, _ in groups[:g])
        copies = []
        for count in range(first_peer, first_peer + groups[g][0] - 1):
            copy = pltpu.make_async_remote_copy(
                red_src.at[g], red_dst.at[count], red_ssem.at[count], red_rsem.at[count],
                device_id=(peers[count],), device_id_type=MESH,
            )
            copy.start()
            copies.append((count, copy))
        rounds.append(copies)

    def start_sums():
        sums = [jnp.sum(macc[i], axis=0, keepdims=True) for i in range(4)]
        send_sums(0, jnp.concatenate(sums + [jnp.zeros((4, LANES), F32)], axis=0))

    moves2 = []
    for c, (r0, size) in enumerate(chunks):
        rows = pl.ds(r0, size)
        for copy in moves1[c]:
            copy.wait_recv()
        for base, mine, theirs in ((0, own1, recv_l1), (OWNED, ahead1, recv_r1)):
            for row in range(OWNED):
                s = base + row
                weight = prior[pl.ds(s, 1), :]
                image = mine[row, rows, :] + theirs[row, rows, :] + weight * zz[s, rows, :]
                w = image * inv[s, rows, :]
                if base == 0:
                    az[s, rows, :] = image
                    ww[s, rows, :] = w
                    macc[2] += fold(image * w)
                    macc[3] += fold(weight * (w * w))
                spread(s, size, w)
        apply_pairs(rows, size, 3, start_sums if c == len(chunks) - 1 else None)
        for base, buf in ((0, own2), (OWNED, ahead2)):
            for s in range(OWNED):
                buf[s, rows, :] = scene_total(base + s, size)
        moves = transfers(c, (r0, size), (ahead2, recv_l2), None, sem_s2, sem_r2)
        for copy in moves:
            copy.start()
        moves2.append(moves)

    for g in range(len(groups)):
        if g > 0:
            send_sums(g, tile)
        tile = red_src[g]
        for count, copy in rounds[g]:
            copy.wait()
            tile = tile + red_dst[count]
    tile = jnp.sum(tile, axis=1, keepdims=True)
    m0, m1, m2, m3 = (tile[i : i + 1, :] for i in range(4))
    first = m0 / m1
    ratio = first * m2 / m1
    again = (ratio - 1.0) * m0
    second = again / (ratio * (ratio * m1 - 2.0 * first * m2) + first * first * m3)
    of_z = first + second * ratio
    of_w = -second * first

    for c, (r0, size) in enumerate(chunks):
        for copy in moves2[c]:
            copy.wait_recv()
        half = size // 2
        low = low_lanes(half)
        for s in range(OWNED):
            weight = prior[pl.ds(s, 1), :]
            parts = []
            for odd in range(2):
                rows = pl.ds(r0 + odd, half, stride=2)
                w = ww[s, rows, :]
                last_image = own2[s, rows, :] + recv_l2[s, rows, :] + weight * w
                parts.append(
                    (
                        of_z * zz[s, rows, :] + of_w * w,
                        res[s, rows, :] - of_z * az[s, rows, :] - of_w * last_image,
                    )
                )
            for out, even, odd in ((out_s, parts[0][0], parts[1][0]), (out_r, parts[0][1], parts[1][1])):
                out[pl.ds((r0 // 2) * OWNED + s, half, stride=OWNED), :] = jnp.where(low, even, swap(odd))
                out[pl.ds((bands // 2 + r0 // 2) * OWNED + s, half, stride=OWNED), :] = jnp.where(low, swap(even), odd)

    for moves in moves0 + moves1 + moves2:
        for copy in moves:
            copy.wait_send()


def shards(n, first_scene, second_scene, rad_first, rad_second, pos_first, pos_second, prior_weight):
    pairs, bands = rad_first.shape[:2]
    halfs = 2 * pairs
    chunks = row_chunks(bands)
    most = max(size for _, size in chunks)
    peers = sum(size - 1 for size, _ in groups_of(n))
    smem = pl.BlockSpec(memory_space=pltpu.SMEM)
    vmem = pl.BlockSpec(memory_space=pltpu.VMEM)
    hbm = pl.BlockSpec(memory_space=pl.ANY)

    def block(rows):
        return pltpu.VMEM((rows, bands, LANES), F32)

    flat = jax.ShapeDtypeStruct((bands * OWNED, LANES), F32)
    outs = pl.pallas_call(
        functools.partial(kernel, n),
        out_shape=(pltpu.VMEM(flat.shape, F32), pltpu.VMEM(flat.shape, F32)),
        in_specs=[smem, smem, smem, hbm, hbm, vmem, vmem],
        out_specs=(vmem, vmem),
        scratch_shapes=[
            pltpu.VMEM((pairs, bands, LANES), BF16),
            pltpu.VMEM((pairs, bands, LANES), BF16),
            pltpu.VMEM((TERMS * pairs, LANES), F32),
            pltpu.VMEM((TERMS * pairs, LANES), F32),
            pltpu.VMEM((pairs, 2 * TERMS, 2 * LANES), BF16),
            pltpu.VMEM((pairs, 4 * TERMS, LANES), BF16),
            pltpu.VMEM((pairs, 4 * TERMS, LANES), BF16),
            pltpu.VMEM((halfs + 1, 2, most, LANES), F32),
            pltpu.VMEM((halfs + 1, most, LANES), F32),
            pltpu.VMEM((halfs + 1, 8, LANES), F32),
            pltpu.VMEM((2 * OWNED, 2, most, LANES), BF16),
            pltpu.VMEM((pairs, most, LANES), F32),
            block(12), block(12), block(12), block(12),
            block(8), block(8), block(8), block(8),
            block(8), block(8), block(8),
            pltpu.VMEM((2 * OWNED, LANES), F32),
            pltpu.VMEM((OWNED, LANES), F32),
            pltpu.VMEM((OWNED, LANES), F32),
            pltpu.VMEM((2 * OWNED, LANES), F32),
            block(8), block(16), block(16), block(8), block(8),
            pltpu.VMEM((2 * OWNED, LANES), F32),
            pltpu.VMEM((2 * OWNED, LANES), F32),
            pltpu.VMEM((4, 8, LANES), F32),
            pltpu.VMEM((len(groups_of(n)), 8, LANES), F32),
            pltpu.VMEM((peers, 8, LANES), F32),
            pltpu.SMEM((halfs,), jnp.int32),
            pltpu.SMEM((halfs,), jnp.int32),
            pltpu.SMEM((2 * OWNED,), jnp.int32),
            pltpu.SemaphoreType.DMA((2 * len(chunks),)),
            pltpu.SemaphoreType.DMA((2 * len(chunks),)),
            pltpu.SemaphoreType.DMA((2 * len(chunks),)),
            pltpu.SemaphoreType.DMA((2 * len(chunks),)),
            pltpu.SemaphoreType.DMA((2 * len(chunks),)),
            pltpu.SemaphoreType.DMA((2 * len(chunks),)),
            pltpu.SemaphoreType.DMA((4,)),
            pltpu.SemaphoreType.DMA((2,)),
            pltpu.SemaphoreType.DMA((peers,)),
            pltpu.SemaphoreType.DMA((peers,)),
        ],
        compiler_params=pltpu.CompilerParams(
            collective_id=0, has_side_effects=True, vmem_limit_bytes=56 * 1024 * 1024
        ),
    )(first_scene, second_scene, prior_weight, rad_first, rad_second, pos_first, pos_second)
    return tuple(
        x.reshape(bands, OWNED, LANES).transpose(1, 0, 2).reshape(OWNED, bands * LANES) for x in outs
    )


def solution(mesh):
    return jax.shard_map(
        functools.partial(shards, mesh.shape["scene"]),
        mesh=mesh,
        in_specs=(
            P("scene"),
            P("scene"),
            P("scene", None, None),
            P("scene", None, None),
            P("scene", None),
            P("scene", None),
            P("scene"),
        ),
        out_specs=(P("scene", None), P("scene", None)),
        check_vma=False,
    )
```
